32 devices in a mesh: wide: 16 (over z, y, x), narrow: 2 (over core).
Axes of the slice: x: 2, y: 2, z: 4, core: 2. Of those that a mesh axis runs over, the one named last changes fastest.
Arguments:
- residual: bfloat16 [64, 16384], P('narrow', 'wide'), may hold values from -54 to 54
- norm_gain: bfloat16 [16384], P('wide'), may hold values from 0.5 to 1.5
- w_query: bfloat16 [16384, 16384], P('wide', 'narrow'), may hold values from -0.046875 to 0.046875
- w_keyval: bfloat16 [16384, 2, 1024], P('wide', None, 'narrow'), may hold values from -0.046875 to 0.046875
- w_out: bfloat16 [16384, 16384], P('narrow', 'wide'), may hold values from -0.375 to 0.375
- cache_rows: bfloat16 [64, 768, 2, 1024], P('wide', None, None, 'narrow'), may hold values from -106 to 106, as said below
- lengths: int32 [64], replicated, may hold values from 1 to 768, 12288 in all
- assignment: int32 [64], replicated, may hold values from 0 to 63, each once
Outputs:
- layer_out: bfloat16 [64, 16384], P('narrow', 'wide')
The draws below stay inside these ranges and needn't reach their ends.
Inputs may be any that keep to these rules, and one draw needn't show every extreme that they name: `lengths`: largest entry reaches 768. `assignment`: each row named once. `cache_rows`: entries at positions at or beyond a row's length are not read.
All inputs are finite; a program needn't handle non-finite values.
Results may differ from the reference program's by a relative error of at most 0.012.
The reference program's roundings to bfloat16 on the way (of `normed`, `queries`, `probs` and `attended`) count: a program that leaves them out, or rounds other values in their place, can miss the bound.
Values may be sent and summed in bfloat16 or wider, within the bound.
No kernel may reach another device: no remote copies, remote signals or barrier semaphores. Data moves between devices by JAX's collectives and lax.ppermute only.
A program may use at most 128 MiB of HBM per device.

```python
import math
import jax
import jax.numpy as jnp
import numpy as np
from jax import lax

D = 16384
H = 128
KVH = 8
HD = 128
MEAN_LEN = 192
ROWS = 64
MOST = 768


def draw_residual(key, part):
    first, second, third = jax.random.split(jax.random.fold_in(key, 11), 3)
    jitter = jnp.clip(jax.random.normal(first, (ROWS, D), jnp.float32), -4.0, 4.0)
    rising = 3.0 ** (jnp.arange(D, dtype=jnp.float32) / D - 0.5)
    column_scale = jnp.exp(jax.random.uniform(second, (D,), jnp.float32, -0.8, 0.8)) * rising
    row_scale = jnp.exp(jax.random.uniform(third, (ROWS, 1), jnp.float32, -0.693, 0.693))
    return (jitter * column_scale[None, :] * row_scale).astype(jnp.bfloat16)


def draw_cache_rows(key, part):
    first = jax.random.fold_in(jax.random.fold_in(key, 23), 0)
    stored = jnp.clip(jax.random.normal(first, (ROWS, MOST, 2, KVH * HD), jnp.float32), -5.0, 5.0)
    return stored.astype(jnp.bfloat16)


def level_of(key, shape, pieces, least, top_value):
    level, own = 1.0, jax.random.fold_in(key, 6)
    for dim, parts in pieces:
        steps = jnp.exp(jax.random.uniform(jax.random.fold_in(own, dim), (parts,), jnp.float32, least / len(pieces), top_value / len(pieces)))
        level = level * jnp.repeat(steps, shape[dim] // parts).reshape([-1 if axis == dim else 1 for axis in range(len(shape))])
    return level


def profile(count, total, most, slope):
    loads = [(1 << 20) // math.isqrt(rank ** slope) + 1 for rank in range(2, count + 1)]
    rest, holding = total - most - (count - 1), [1] * (count - 1)
    while rest > 0:
        candidates = [i for i in range(count - 1) if holding[i] < most]
        whole, budget = sum([loads[i] for i in candidates]), rest
        for i in candidates:
            more = min(most - holding[i], max(1, budget * loads[i] // whole), rest)
            holding[i] = holding[i] + more
            rest = rest - more
    return np.array([most] + holding)


def ragged(rng, number_of, total, most, slope):
    if number_of == 2:
        one = jax.random.randint(rng, (), max(1, total - most), min(most, total - 1) + 1)
        return jnp.stack([one, total - one])
    sizes = jnp.asarray(profile(number_of, total, most, slope), jnp.int32)
    twos = (number_of - 1) // 2
    donor, receiver = sizes[1:1 + 2 * twos:2], sizes[2:2 + 2 * twos:2]
    margin = jnp.minimum(donor - 1, most - receiver)
    moved = jax.random.randint(jax.random.fold_in(rng, 1), (twos,), 0, 1 << 20) % (margin + 1)
    sizes = sizes.at[1:1 + 2 * twos:2].set(donor - moved).at[2:2 + 2 * twos:2].set(receiver + moved)
    return sizes[jax.random.permutation(jax.random.fold_in(rng, 2), number_of)]


def gaussian(stream_key, dims, spread, reach, shards=(), kind=jnp.bfloat16):
    result = jax.random.normal(stream_key, dims, jnp.float32) * spread
    if len(shards) > 0:
        result = level_of(stream_key, dims, shards, -0.22, 0.18) * result
    return jnp.clip(result, min=-reach, max=reach).astype(kind)


def setup_inputs(seed: int = 0) -> dict:
    streams_of = jax.random.split(jax.random.key(seed), 9)
    residual = draw_residual(jax.random.fold_in(streams_of[8], 71), 0)
    norm_gain = jnp.clip(1.0 + 0.1 * jax.random.normal(streams_of[1], (D,), jnp.float32), 0.5, 1.5).astype(jnp.bfloat16)
    w_query = gaussian(streams_of[2], (D, H * HD), D ** -0.5, 0.046875, ((0, 16), (1, 2)))
    w_keyval = gaussian(streams_of[3], (D, 2, KVH * HD), D ** -0.5, 0.046875, ((0, 16), (2, 2)))
    w_out = gaussian(streams_of[4], (H * HD, D), (H * HD // 64) ** -0.5, 0.375, ((0, 2), (1, 16)))
    cache_rows = draw_cache_rows(jax.random.fold_in(streams_of[8], 71), 0)
    lengths = ragged(streams_of[6], ROWS, ROWS * MEAN_LEN, MOST, 2).astype(jnp.int32)
    assignment = jax.random.permutation(streams_of[7], ROWS).astype(jnp.int32)
    return {"residual": residual, "norm_gain": norm_gain, "w_query": w_query, "w_keyval": w_keyval, "w_out": w_out, "cache_rows": cache_rows, "lengths": lengths, "assignment": assignment}


def rotate(values, positions):
    half_dim = values.shape[-1] // 2
    freqs = 500000.0 ** (-(jnp.arange(half_dim, dtype=jnp.float32) * 2.0 / values.shape[-1]))
    angles = positions[..., None] * freqs
    cosine = jnp.cos(angles)
    sine = jnp.sin(angles)
    first_half = values[..., :half_dim]
    second_half = values[..., half_dim:]
    return jnp.concatenate([first_half * cosine - second_half * sine, second_half * cosine + first_half * sine], axis=-1)

def reference(residual, norm_gain, w_query, w_keyval, w_out, cache_rows, lengths, assignment):
    inputs = residual.astype(jnp.float32)
    inverse_rms = lax.rsqrt(lax.optimization_barrier(jnp.mean(inputs * inputs, axis=1, keepdims=True)) + 1e-05)
    normed = (inputs * inverse_rms * norm_gain.astype(jnp.float32)).astype(jnp.bfloat16)
    query_raw = jnp.dot(normed, w_query, preferred_element_type=jnp.float32)
    keyval_raw = jnp.dot(normed, w_keyval.reshape(D, 2 * KVH * HD), preferred_element_type=jnp.float32)
    keyval_raw = keyval_raw.reshape(ROWS, 2, KVH, HD)
    positions = lengths.astype(jnp.float32)[:, None]
    queries = rotate(query_raw.reshape(ROWS, H, HD), positions).astype(jnp.bfloat16)
    keys_new = rotate(keyval_raw[:, 0], positions).astype(jnp.bfloat16)
    values_new = keyval_raw[:, 1].astype(jnp.bfloat16)
    slot_of = jnp.zeros((ROWS,), jnp.int32).at[assignment].set(jnp.arange(ROWS, dtype=jnp.int32))
    group_size = H // KVH
    scale = 1.0 / math.sqrt(HD)

    def attend_row(row_id):
        slot_id = slot_of[row_id]
        stored = lax.dynamic_index_in_dim(cache_rows, slot_id, 0, keepdims=False).astype(jnp.float32)
        keys = stored[:, 0].reshape(MOST, KVH, HD)
        values = stored[:, 1].reshape(MOST, KVH, HD)
        query = queries[row_id].astype(jnp.float32).reshape(KVH, group_size, HD)
        scores = jnp.einsum('kgd,jkd->kgj', query, keys) * scale
        live_mask = jnp.arange(MOST, dtype=jnp.int32) < lengths[row_id]
        scores = jnp.where(live_mask[None, None, :], scores, -jnp.inf)
        own_score = jnp.einsum('kgd,kd->kg', query, keys_new[row_id].astype(jnp.float32)) * scale
        maxima = jnp.maximum(lax.optimization_barrier(jnp.max(scores, axis=-1)), own_score)
        weights = jnp.exp(scores - maxima[..., None])
        own_weight = jnp.exp(own_score - maxima)
        totals = lax.optimization_barrier(jnp.sum(weights, axis=-1)) + own_weight
        probs = lax.optimization_barrier((weights / totals[..., None]).astype(jnp.bfloat16)).astype(jnp.float32)
        own_prob = lax.optimization_barrier((own_weight / totals).astype(jnp.bfloat16)).astype(jnp.float32)
        attended = jnp.einsum('kgj,jkd->kgd', probs, values)
        attended = attended + own_prob[..., None] * values_new[row_id].astype(jnp.float32)[:, None, :]
        return attended.reshape(H * HD).astype(jnp.bfloat16)
    attended_rows = lax.map(attend_row, jnp.arange(ROWS, dtype=jnp.int32))
    update = jnp.dot(attended_rows, w_out, preferred_element_type=jnp.float32)
    return (inputs + update).astype(jnp.bfloat16)
```

```python
import functools
import math

import jax
import jax.numpy as jnp
from jax import lax
from jax.experimental import pallas as pl
from jax.experimental.pallas import tpu as pltpu
from jax.sharding import PartitionSpec as P

HD = 128
BF = jnp.bfloat16
F32 = jnp.float32
VMEM_LIMIT = 48 * 1024 * 1024
NT = (((1,), (1,)), ((), ()))


def params(**kw):
    return pltpu.CompilerParams(vmem_limit_bytes=VMEM_LIMIT, **kw)


def log2(n):
    return n.bit_length() - 1


def split_hi_lo(value):
    hi = value.astype(BF)
    return hi, (value - hi.astype(F32)).astype(BF)


def slot_of_row(rel, me, slots, order):
    block = lax.shift_right_logical(rel, log2(slots))
    count = len(order)
    mask = jnp.zeros_like(rel)
    for k, bit in enumerate(order):
        on = lax.bitwise_and(lax.shift_right_logical(rel, log2(slots) + count - 1 - k), 1)
        mask = mask + on * bit
    del block
    return lax.bitwise_xor(mask, me) * slots + lax.bitwise_and(rel, slots - 1)


def one_hot(condition):
    return jnp.where(condition, 1.0, 0.0).astype(BF)


def project_kernel(me_ref, assign_ref, x_ref, gain_ref, w_ref, *rest, slots, order, with_kv):
    if with_kv:
        wkv_ref, keep_ref, send_ref, keep2_ref, send2_ref, lhs = rest
    else:
        keep_ref, send_ref, lhs = rest
    rows = x_ref.shape[0]
    half = rows // 2

    @pl.when(pl.program_id(0) == 0)
    def _():
        rel = lax.broadcasted_iota(jnp.int32, (rows, rows), 0)
        col = lax.broadcasted_iota(jnp.int32, (rows, rows), 1)
        pick = one_hot(slot_of_row(rel, me_ref[0], slots, order) == col)
        named = one_hot(rel == assign_ref[...])
        perm = lax.dot_general(pick, named, NT, preferred_element_type=F32).astype(BF)
        mine = jnp.dot(perm, x_ref[...], preferred_element_type=F32)
        scaled = mine * gain_ref[...].astype(F32)
        hi, lo = split_hi_lo(scaled)
        lhs[:rows, :] = hi
        lhs[rows:, :] = lo
        if with_kv:
            kv = wkv_ref.shape[1]
            both = jnp.dot(lhs[...], wkv_ref[...], preferred_element_type=F32)
            both = both[:rows] + both[rows:]
            keep2_ref[:, :kv] = both[:half]
            send2_ref[:, :kv] = both[half:].astype(BF)
            squares = jnp.sum(mine * mine, axis=1, keepdims=True)
            wide = jnp.broadcast_to(squares, (rows, HD))
            keep2_ref[:, kv : kv + HD] = wide[:half]
            hi, lo = split_hi_lo(wide[half:])
            send2_ref[:, kv : kv + HD] = hi
            send2_ref[:, kv + HD :] = lo

    both = jnp.dot(lhs[...], w_ref[...], preferred_element_type=F32)
    both = both[:rows] + both[rows:]
    keep_ref[...] = both[:half]
    send_ref[...] = both[half:].astype(BF)


def project(me, assignment, x, gain, w, piece, pieces, slots, order, wkv=None):
    rows, depth = x.shape
    cols = w.shape[1] // pieces
    tile = min(1024, cols)
    steps = cols // tile
    half = rows // 2
    whole = lambda a: pl.BlockSpec(a.shape, lambda i: (0,) * a.ndim)
    ins = [me, assignment, x, gain, w]
    in_specs = [
        pl.BlockSpec(memory_space=pltpu.SMEM),
        whole(assignment),
        whole(x),
        whole(gain),
        pl.BlockSpec((depth, tile), lambda i: (0, piece * steps + i)),
    ]
    shapes = [jax.ShapeDtypeStruct((half, cols), F32), jax.ShapeDtypeStruct((half, cols), BF)]
    out_specs = [
        pl.BlockSpec((half, tile), lambda i: (0, i)),
        pl.BlockSpec((half, tile), lambda i: (0, i)),
    ]
    if wkv is not None:
        ins.append(wkv)
        in_specs.append(whole(wkv))
        extra = [
            jax.ShapeDtypeStruct((half, wkv.shape[1] + HD), F32),
            jax.ShapeDtypeStruct((half, wkv.shape[1] + 2 * HD), BF),
        ]
        shapes += extra
        out_specs += [whole(a) for a in extra]
    return pl.pallas_call(
        functools.partial(project_kernel, slots=slots, order=order, with_kv=wkv is not None),
        grid=(steps,),
        in_specs=in_specs,
        out_specs=out_specs,
        out_shape=shapes,
        scratch_shapes=[pltpu.VMEM((2 * rows, depth), BF)],
        compiler_params=params(),
        cost_estimate=pl.CostEstimate(
            flops=4 * rows * depth * cols, bytes_accessed=2 * depth * cols, transcendentals=0
        ),
    )(*ins)


def add_kernel(keep_ref, recv_ref, *outs, parts, squares):
    cols = keep_ref.shape[1] - (HD if squares else 0)
    rows = keep_ref.shape[0] // parts
    total = keep_ref[:, :cols] + recv_ref[:, :cols].astype(F32)
    if squares:
        sq = keep_ref[:, cols:] + (
            recv_ref[:, cols : cols + HD].astype(F32) + recv_ref[:, cols + HD :].astype(F32)
        )
    for part in range(parts):
        here = slice(part * rows, (part + 1) * rows)
        out = outs[part]
        out[:, :cols] = total[here].astype(out.dtype)
        if squares:
            if part == 0:
                out[:, cols:] = sq[here]
            else:
                hi, lo = split_hi_lo(sq[here])
                out[:, cols : cols + HD] = hi
                out[:, cols + HD :] = lo


def add_split(keep, recv, parts, squares):
    rows = keep.shape[0] // parts
    shapes = [jax.ShapeDtypeStruct((rows, keep.shape[1]), F32)]
    shapes += [jax.ShapeDtypeStruct((rows, recv.shape[1]), BF)] * (parts - 1)
    return pl.pallas_call(
        functools.partial(add_kernel, parts=parts, squares=squares),
        out_shape=shapes,
        in_specs=[pl.BlockSpec(memory_space=pltpu.VMEM)] * 2,
        out_specs=[pl.BlockSpec(memory_space=pltpu.VMEM)] * parts,
        compiler_params=params(),
    )(keep, recv)


def exchange(value, axis, bit):
    n = lax.axis_size(axis)
    return lax.ppermute(value, axis, [(i, i ^ bit) for i in range(n)])


def direct_masks(order):
    return [order[-1], order[-2], order[-1] | order[-2]]


def attend_kernel(
    me_ref, lengths_ref, assign_ref, cos_ref, sin_ref, gathered, k_ref, v_ref, out_ref,
    raw, queries, kv_new, result, *, slots, groups, group_size, pieces, width, kv_cols,
):
    step = pl.program_id(0)
    heads = groups * group_size
    head_cols = heads * HD // pieces
    scale = 1.0 / math.sqrt(HD)

    @pl.when(step == 0)
    def _():
        for p in range(pieces):
            keep, *parts = gathered[p]
            total = keep[...]
            for part in parts:
                total = total + part[...].astype(F32)
            for h in range(heads // pieces):
                raw[pl.ds((p * (heads // pieces) + h) * 8, slots), :] = total[
                    :, h * HD : (h + 1) * HD
                ]
        keep, *parts = gathered[pieces]
        total = keep[:, :kv_cols]
        squares = keep[:, kv_cols:]
        for part in parts:
            total = total + part[:, :kv_cols].astype(F32)
            squares = squares + (
                part[:, kv_cols : kv_cols + HD].astype(F32) + part[:, kv_cols + HD :].astype(F32)
            )
        inverse = lax.rsqrt(squares / width + 1e-05)
        for h in range(2 * groups):
            kv_new[h] = total[:, h * HD : (h + 1) * HD] * inverse
        kv_new[2 * groups] = inverse

    def pick(value):
        return value

    length = lengths_ref[assign_ref[me_ref[0] * slots + step]]
    cosine = cos_ref[pl.ds(step, 1), :]
    sine = sin_ref[pl.ds(step, 1), :]
    inverse = kv_new[2 * groups, pl.ds(step, 1), :]
    most = k_ref.shape[2]
    live = lax.broadcasted_iota(jnp.int32, (group_size, most), 1) < length

    def rotate(value):
        return value * cosine + pltpu.roll(value, HD // 2, 1) * sine

    for g in range(groups):
        here = slice(g * HD, (g + 1) * HD)
        query = raw[pl.ds(g * group_size * 8 + step, group_size, stride=8), :] * inverse
        query = rotate(query).astype(BF)
        k_new = rotate(kv_new[g, pl.ds(step, 1), :]).astype(BF).astype(F32)
        v_new = kv_new[groups + g, pl.ds(step, 1), :].astype(BF).astype(F32)
        own = jnp.sum(query.astype(F32) * k_new, axis=1, keepdims=True) * scale
        scores = (
            lax.dot_general(query, k_ref[0, 0, :, here], NT, preferred_element_type=F32) * scale
        )
        scores = jnp.where(live, scores, -jnp.inf)
        top = jnp.maximum(jnp.max(scores, axis=1, keepdims=True), own)
        weights = jnp.exp(scores - top)
        own = jnp.exp(own - top)
        total = jnp.sum(weights, axis=1, keepdims=True) + own
        probs = (weights / total).astype(BF)
        own = (own / total).astype(BF).astype(F32)
        summed = jnp.dot(probs, v_ref[0, 0, :, here], preferred_element_type=F32) + own * v_new
        result[pl.ds(g * group_size * 8 + step, group_size, stride=8), :] = summed

    @pl.when(step == slots - 1)
    def _():
        for p in range(pieces):
            for h in range(heads // pieces):
                out_ref[p][:, h * HD : (h + 1) * HD] = result[
                    pl.ds((p * (heads // pieces) + h) * 8, slots), :
                ].astype(BF)
    del queries, head_cols, pick


def attend(me, lengths, assignment, cosine, sine, gathered, cache, slots, groups, heads, width):
    pieces = len(gathered) - 1
    most, channels = cache.shape[2], cache.shape[3]
    counts = [len(g) for g in gathered]
    flat = [a for g in gathered for a in g]
    kv_cols = 2 * groups * HD

    def kernel(me_ref, lengths_ref, assign_ref, cos_ref, sin_ref, *rest):
        refs, rest = rest[: len(flat)], rest[len(flat) :]
        nested, at = [], 0
        for c in counts:
            nested.append(refs[at : at + c])
            at += c
        k_ref, v_ref = rest[0], rest[1]
        outs = rest[2 : 2 + pieces]
        attend_kernel(
            me_ref, lengths_ref, assign_ref, cos_ref, sin_ref, nested, k_ref, v_ref, outs,
            *rest[2 + pieces :], slots=slots, groups=groups, group_size=heads // groups,
            pieces=pieces, width=width, kv_cols=kv_cols,
        )

    smem = pl.BlockSpec(memory_space=pltpu.SMEM)
    whole = lambda a: pl.BlockSpec(a.shape, lambda i: (0,) * a.ndim)
    cols = heads * HD // pieces
    outs = [jax.ShapeDtypeStruct((slots, cols), BF)] * pieces
    return pl.pallas_call(
        kernel,
        grid=(slots,),
        in_specs=[smem, smem, smem, whole(cosine), whole(sine)]
        + [whole(a) for a in flat]
        + [
            pl.BlockSpec((1, 1, most, channels), lambda i: (i, 0, 0, 0)),
            pl.BlockSpec((1, 1, most, channels), lambda i: (i, 1, 0, 0)),
        ],
        out_specs=[whole(a) for a in outs],
        out_shape=outs,
        scratch_shapes=[
            pltpu.VMEM((heads * 8, HD), F32),
            pltpu.VMEM((8, HD), F32),
            pltpu.VMEM((2 * groups + 1, slots, HD), F32),
            pltpu.VMEM((heads * 8, HD), F32),
        ],
        compiler_params=params(),
    )(me, lengths, assignment, cosine, sine, *flat, cache, cache)


def output_kernel(me_ref, other_ref, assign_ref, *rest, counts, slots, order, row_block, first):
    parts, rest = rest[:counts], rest[counts:]
    if first:
        w_ref, out_ref, lhs = rest
    else:
        before_ref, w_ref, out_ref, lhs = rest
    rows = out_ref.shape[0]
    tile = w_ref.shape[0]
    step = pl.program_id(0)

    @pl.when(step == 0)
    def _():
        out_row = lax.broadcasted_iota(jnp.int32, (rows, rows), 0)
        col = lax.broadcasted_iota(jnp.int32, (rows, rows), 1)
        block = lax.bitwise_xor(lax.shift_right_logical(out_row, log2(row_block)), other_ref[0])
        row = block * row_block + lax.bitwise_and(out_row, row_block - 1)
        named = one_hot(row == assign_ref[...])
        pick = one_hot(slot_of_row(out_row, me_ref[0], slots, order) == col)
        perm = lax.dot_general(named, pick, NT, preferred_element_type=F32).astype(BF)
        at = 0
        total = None
        for part in parts:
            n = part.shape[0]
            term = jnp.dot(perm[:, at : at + n], part[...], preferred_element_type=F32)
            total = term if total is None else total + term
            at += n
        total = total.astype(BF)
        for k in range(lhs.shape[0]):
            lhs[k] = total[:, k * tile : (k + 1) * tile]
        out_ref[...] = jnp.zeros_like(out_ref) if first else before_ref[...]

    out_ref[...] += jnp.dot(lhs[step], w_ref[...], preferred_element_type=F32)


def output(me, other, assignment, parts, w, piece, pieces, slots, order, row_block, before=None):
    rows = sum(a.shape[0] for a in parts)
    depth = w.shape[0] // pieces
    tile = min(1024, depth)
    steps = depth // tile
    smem = pl.BlockSpec(memory_space=pltpu.SMEM)
    whole = lambda a: pl.BlockSpec(a.shape, lambda i: (0,) * a.ndim)
    out = jax.ShapeDtypeStruct((rows, w.shape[1]), F32)
    ins = [me, other, assignment, *parts] + ([] if before is None else [before]) + [w]
    in_specs = [smem, smem, whole(assignment)] + [whole(a) for a in parts]
    if before is not None:
        in_specs.append(whole(before))
    in_specs.append(pl.BlockSpec((tile, w.shape[1]), lambda i: (piece * steps + i, 0)))
    return pl.pallas_call(
        functools.partial(
            output_kernel, counts=len(parts), slots=slots, order=order, row_block=row_block,
            first=before is None,
        ),
        grid=(steps,),
        in_specs=in_specs,
        out_specs=whole(out),
        out_shape=out,
        scratch_shapes=[pltpu.VMEM((steps, rows, tile), BF)],
        compiler_params=params(),
        cost_estimate=pl.CostEstimate(
            flops=2 * rows * depth * w.shape[1],
            bytes_accessed=2 * depth * w.shape[1],
            transcendentals=0,
        ),
    )(*ins)


def angles_of(positions):
    half = HD // 2
    freqs = 500000.0 ** (-(jnp.arange(half, dtype=F32) * 2.0 / HD))
    angles = positions[:, None] * freqs
    cosine, sine = jnp.cos(angles), jnp.sin(angles)
    return jnp.concatenate([cosine, cosine], 1), jnp.concatenate([-sine, sine], 1)


def per_device(residual, norm_gain, w_query, w_keyval, w_out, cache_rows, lengths, assignment):
    n = lax.axis_size("wide")
    slots, most, _, channels = cache_rows.shape
    groups = channels // HD
    heads = w_query.shape[1] // HD
    depth = w_query.shape[0]
    width = depth * n
    row_block = residual.shape[0]
    narrow = lax.axis_size("narrow")
    pieces = 2 if groups % 2 == 0 else 1
    bits = [1 << k for k in range(log2(n))]
    top = bits[2:][::-1]
    orders = [[bits[0], bits[1]] + top, [bits[1], bits[0]] + top][:pieces]

    me = lax.axis_index("wide").astype(jnp.int32)
    me1 = me.reshape(1)
    other1 = lax.axis_index("narrow").astype(jnp.int32).reshape(1)
    named = assignment.reshape(1, -1)
    gathered = lax.all_gather(residual, "narrow", axis=0, tiled=True)
    gain = norm_gain.reshape(1, -1)
    wkv = w_keyval.reshape(depth, 2 * channels)

    state = []
    for p in range(pieces):
        last = p == pieces - 1
        got = project(
            me1, named, gathered, gain, w_query, p, pieces, slots, orders[p], wkv if last else None
        )
        state.append([got[0], got[1], orders[p], False])
        if last:
            state.append([got[2], got[3], orders[p], True])

    for stage in range(len(bits) - 2):
        received = [exchange(send, "wide", order[stage]) for _, send, order, _ in state]
        final = stage == len(bits) - 3
        for k, (keep, _, order, squares) in enumerate(state):
            outs = add_split(keep, received[k], 4 if final else 2, squares)
            state[k] = [outs[0], outs[1:] if final else outs[1], order, squares]
    arrived = []
    for keep, sends, order, _ in state:
        masks = direct_masks(order)
        arrived.append([keep] + [exchange(s, "wide", m) for s, m in zip(sends, masks)])

    cache = jnp.transpose(cache_rows, (0, 2, 1, 3))
    owned = lax.dynamic_slice_in_dim(assignment, me * slots, slots)
    cosine, sine = angles_of(lengths[owned].astype(F32))
    attended = attend(
        me1, lengths, assignment, cosine, sine, arrived, cache, slots, groups, heads, width
    )

    blocks = []
    for p in range(pieces):
        own = attended[p]
        blocks.append(
            [jnp.concatenate([own] + [exchange(own, "wide", m) for m in direct_masks(orders[p])], 0)]
        )
    for stage in reversed(range(len(bits) - 2)):
        for p in range(pieces):
            have = blocks[p][0] if len(blocks[p]) == 1 else jnp.concatenate(blocks[p], 0)
            blocks[p] = blocks[p] + [exchange(have, "wide", orders[p][stage])]
    update = None
    for p in range(pieces):
        update = output(
            me1, other1, named, blocks[p], w_out, p, pieces, slots, orders[p], row_block, update
        )
    bit = narrow // 2
    while bit >= 1:
        half = update.shape[0] // 2
        update = update[:half] + exchange(update[half:], "narrow", bit)
        bit //= 2
    return (residual.astype(F32) + update).astype(BF)


def solution(mesh):
    placed = (
        P("narrow", "wide"),
        P("wide"),
        P("wide", "narrow"),
        P("wide", None, "narrow"),
        P("narrow", "wide"),
        P("wide", None, None, "narrow"),
        P(),
        P(),
    )
    return jax.shard_map(
        per_device, mesh=mesh, in_specs=placed, out_specs=P("narrow", "wide"), check_vma=False
    )
```
